32 devices in a mesh: groups: 2 (over x), owner: 16 (over z, y, core).
Axes of the slice: x: 2, y: 2, z: 4, core: 2. Of those that a mesh axis runs over, the one named last changes fastest.
Arguments:
- embeddings: bfloat16 [65536, 256], P(('groups', 'owner')), parts along dimension 0, may hold values from -6 to 6
- code_one: int32 [65536], P(('groups', 'owner')), parts along dimension 0, may hold values from 0 to 127, as said below
- code_two: int32 [65536], P(('groups', 'owner')), parts along dimension 0, may hold values from 0 to 1023
- parent_slot: int32 [256], P('groups'), parts along dimension 0, may hold values from 0 to 127, as said below
- centers_one: float32 [256, 256], P('groups'), parts along dimension 0, may hold values from -6 to 6
- centers_two: bfloat16 [256, 1024, 256], P(('groups', 'owner')), parts along dimension 0, may hold values from -6 to 6
Outputs:
- new_one: float32 [256, 256], P('groups'), parts along dimension 0
- new_two: bfloat16 [256, 1024, 256], P(('groups', 'owner')), parts along dimension 0
- residual_two: bfloat16 [65536, 256], P(('groups', 'owner')), parts along dimension 0
The draws below stay inside these ranges and needn't reach their ends.
There are 2 independent parts, one for each index of `groups`. The reference program is written for one: setup_inputs(seed, part) draws one part's arguments, and reference() takes and returns one part's arrays. A program takes and returns all parts, laid end to end along the dimension named above; each array names one. Nothing has to cross between parts.
Inputs may be any that keep to these rules, and one draw needn't show every extreme that they name: A permutation: the codebook of level-1 codeword p is row parent_slot[p] of centers_two. `code_one`: count the codewords p with parent_slot[p] // 8 = o as those of owner o. The 2048 entities of one owner index have at most 256 level-1 codes of any one owner; one owner receives exactly this many from every owner index.
All inputs are finite; a program needn't handle non-finite values.
Results may differ from the reference program's by a relative error of at most 0.0004.
Values may be sent and summed in bfloat16 or wider, within the bound.
A program may use at most 128 MiB of HBM per device.

```python
import jax
import jax.numpy as jnp

D = 256
K2 = 1024
PAR_DEV = 8
ENT_DEV = 2048
OWNERS = 16
PARENTS = 128
ENTITIES = 32768


def shared_slots(key):
    return jax.random.permutation(key, PARENTS).astype(jnp.int32)


def draw_parent_slot(key, part):
    slots = shared_slots(key)
    return slots


def draw_code_one(key, part):
    slots = shared_slots(key)
    key = jax.random.fold_in(key, 2)
    parent_of = jnp.argsort(slots).astype(jnp.int32)
    base_count = ENT_DEV // OWNERS
    hottest = jax.random.randint(jax.random.fold_in(key, 7), (), 0, OWNERS).astype(jnp.int32)

    def one_device(dev_key):
        key_order, key_extra, key_first, key_second, key_shuffle = jax.random.split(dev_key, 5)
        order = jax.random.permutation(key_order, OWNERS).astype(jnp.int32)
        leading = order[0]
        order = jnp.where(order == hottest, leading, order).at[0].set(hottest)
        extra = jax.random.randint(key_extra, (OWNERS // 2,), 0, base_count + 1).astype(jnp.int32)
        extra = extra.at[0].set(base_count)
        counts = jnp.stack([base_count + extra, base_count - extra], 1).reshape(OWNERS)
        bounds = jnp.cumsum(counts)
        positions = jnp.arange(ENT_DEV, dtype=jnp.int32)
        ranked = jnp.searchsorted(bounds, positions, side='right').astype(jnp.int32)
        target = order[ranked]
        local_first = jax.random.randint(key_first, (ENT_DEV,), 0, PAR_DEV)
        local_second = jax.random.randint(key_second, (ENT_DEV,), 0, PAR_DEV)
        local_slot = jnp.minimum(local_first, local_second).astype(jnp.int32)
        parents = parent_of[target * PAR_DEV + local_slot]
        shuffle = jax.random.permutation(key_shuffle, ENT_DEV)
        return parents[shuffle]
    dev_keys = jax.random.split(key, OWNERS)
    return jax.vmap(one_device)(dev_keys).reshape(OWNERS * ENT_DEV).astype(jnp.int32)


def touch_ends(result, rng, least, top_value):
    index_at = [jax.random.randint(jax.random.fold_in(rng, axis), (), 0, length) for axis, length in enumerate(result.shape)]
    longest = result.shape.index(max(result.shape))
    next_to = index_at[:longest] + [(index_at[longest] + 1) % result.shape[longest]] + index_at[longest + 1:]
    return result.at[tuple(index_at)].set(least).at[tuple(next_to)].set(top_value)


def levels(key, extent, shards, smallest, largest):
    loudness, own = 1.0, jax.random.fold_in(key, 6)
    for dim, parts in shards:
        steps = jnp.exp(jax.random.uniform(jax.random.fold_in(own, dim), (parts,), jnp.float32, smallest / len(shards), largest / len(shards)))
        loudness = loudness * jnp.repeat(steps, extent[dim] // parts).reshape([-1 if axis == dim else 1 for axis in range(len(extent))])
    return loudness


def scatter_about(own_key, dims, scale, limit, pieces=(), kind=jnp.bfloat16):
    entries = scale * jax.random.normal(own_key, dims, jnp.float32)
    if pieces:
        entries = entries * levels(own_key, dims, pieces, -0.22, 0.18)
    return jnp.clip(entries, -limit, limit).astype(kind)


def setup_inputs(seed: int = 0, part: int = 0) -> dict:
    key_list = jax.random.split(jax.random.key(seed), 7)
    part_keys = jax.random.split(jax.random.fold_in(key_list[6], part), 7)
    embeddings = scatter_about(part_keys[0], (ENTITIES, D), 1.0, 6.0, ((0, 16),))
    code_one = draw_code_one(jax.random.fold_in(jax.random.fold_in(key_list[6], part), 71), part)
    code_two = touch_ends(jax.random.randint(part_keys[2], (ENTITIES,), 0, K2), jax.random.fold_in(part_keys[2], 1), 0, K2 - 1).astype(jnp.int32)
    parent_slot = draw_parent_slot(jax.random.fold_in(jax.random.fold_in(key_list[6], part), 71), part)
    centers_one = scatter_about(part_keys[4], (PARENTS, D), 1.0, 6.0, (), jnp.float32)
    centers_two = scatter_about(part_keys[5], (PARENTS, K2, D), 1.0, 6.0, ((0, 16),))
    return {"embeddings": embeddings, "code_one": code_one, "code_two": code_two, "parent_slot": parent_slot, "centers_one": centers_one, "centers_two": centers_two}


prior_one = 16.0
prior_two = 1.0


def reference(embeddings, code_one, code_two, parent_slot, centers_one, centers_two):
    values = embeddings.astype(jnp.float32)
    sums_one = jax.ops.segment_sum(values, code_one, num_segments=PARENTS)
    counts_one = jax.ops.segment_sum(jnp.ones(code_one.shape, jnp.float32), code_one, num_segments=PARENTS)
    new_one = (sums_one + prior_one * centers_one) / (counts_one[:, None] + prior_one)
    residual = values - jnp.take(new_one, code_one, axis=0)
    cells = (jnp.take(parent_slot, code_one) * K2 + code_two).astype(jnp.int32)
    sums_two = jax.ops.segment_sum(residual, cells, num_segments=PARENTS * K2)
    counts_two = jax.ops.segment_sum(jnp.ones(cells.shape, jnp.float32), cells, num_segments=PARENTS * K2)
    refined = (sums_two.reshape(PARENTS, K2, D) + prior_two * centers_two.astype(jnp.float32)) / (counts_two.reshape(PARENTS, K2, 1) + prior_two)
    residual_two = (residual - jnp.take(refined.reshape(PARENTS * K2, D), cells, axis=0)).astype(jnp.bfloat16)
    return new_one, refined.astype(jnp.bfloat16), residual_two
```

```python
import functools

import jax
import jax.numpy as jnp
from jax import lax
from jax.experimental import pallas as pl
from jax.experimental.pallas import tpu as pltpu
from jax.sharding import PartitionSpec as P

prior_one = 16.0
prior_two = 1.0
tile = 256
digit_bits = 7
bf16 = jnp.bfloat16
f32 = jnp.float32
i32 = jnp.int32


def iota(shape, axis):
    return lax.broadcasted_iota(i32, shape, axis)


def shift_of(count):
    assert count & (count - 1) == 0
    return count.bit_length() - 1


def one_hot(hits):
    return jnp.where(hits, 1.0, 0.0).astype(bf16)


def dot(left, right):
    return jnp.dot(left, right, preferred_element_type=f32)


def exact_dot(left, right):
    return jnp.dot(left, right, preferred_element_type=f32, precision=lax.Precision.HIGHEST)


def column(row):
    size = row.shape[1]
    same = iota((size, size), 0) == iota((size, size), 1)
    return jnp.sum(jnp.where(same, row, 0), axis=1, keepdims=True)


def as_row(col):
    size = col.shape[0]
    same = iota((size, size), 0) == iota((size, size), 1)
    return jnp.sum(jnp.where(same, col, 0), axis=0, keepdims=True)


def kernel(
    owners,
    books,
    emb,
    code_one,
    code_two,
    slot_col,
    slot_row,
    cent_one,
    cent_two,
    new_one,
    new_two,
    resid,
    pos_row,
    pos_col,
    digits,
    send_codes,
    got_codes,
    cell_col,
    cell_row,
    packed,
    arrived,
    picked,
    shares,
    outgoing,
    returned,
    total,
    own_one,
    all_one,
    code_send,
    code_recv,
    row_send,
    row_recv,
    back_send,
    back_recv,
    one_send,
    one_recv,
):
    me = lax.axis_index("owner")
    rows, width = emb.shape
    parents = cent_one.shape[0]
    cells = cent_two.shape[0]
    words = cells // books
    slots = arrived.shape[0]
    cap = slots // owners
    word_shift = shift_of(words)
    book_shift = shift_of(books)

    def other(k):
        return lax.rem(me + k, owners)

    def block(index, size=cap):
        return pl.ds(pl.multiple_of(index * size, size), size)

    def codes_to(peer):
        return pltpu.make_async_remote_copy(
            src_ref=send_codes.at[peer],
            dst_ref=got_codes.at[me],
            send_sem=code_send.at[peer],
            recv_sem=code_recv.at[me],
            device_id={"owner": peer},
            device_id_type=pl.DeviceIdType.MESH,
        )

    def codes_from(peer):
        return pltpu.make_async_remote_copy(
            src_ref=send_codes.at[me],
            dst_ref=got_codes.at[peer],
            send_sem=code_send.at[me],
            recv_sem=code_recv.at[peer],
            device_id={"owner": peer},
            device_id_type=pl.DeviceIdType.MESH,
        )

    def block_copy(source, landing, send, recv, source_at, landing_at, peer, size=cap):
        return pltpu.make_async_remote_copy(
            src_ref=source.at[block(source_at, size)],
            dst_ref=landing.at[block(landing_at, size)],
            send_sem=send.at[source_at],
            recv_sem=recv.at[landing_at],
            device_id={"owner": peer},
            device_id_type=pl.DeviceIdType.MESH,
        )

    def rows_to(peer):
        return block_copy(packed, arrived, row_send, row_recv, peer, me, peer)

    def rows_from(peer):
        return block_copy(packed, arrived, row_send, row_recv, me, peer, peer)

    def back_to(peer):
        return block_copy(outgoing, returned, back_send, back_recv, peer, me, peer)

    def back_from(peer):
        return block_copy(outgoing, returned, back_send, back_recv, me, peer, peer)

    def one_copy(landing_at, sem_at, peer):
        return pltpu.make_async_remote_copy(
            src_ref=own_one.at[pl.ds(0, books)],
            dst_ref=all_one.at[block(landing_at, books)],
            send_sem=one_send.at[sem_at],
            recv_sem=one_recv.at[landing_at],
            device_id={"owner": peer},
            device_id_type=pl.DeviceIdType.MESH,
        )

    barrier = pltpu.get_barrier_semaphore()

    @pl.loop(1, owners)
    def _(k):
        pl.semaphore_signal(
            barrier, inc=1, device_id={"owner": other(k)}, device_id_type=pl.DeviceIdType.MESH
        )

    upto = one_hot(iota((tile, tile), 0) <= iota((tile, tile), 1))
    offset = jnp.zeros((owners, 1), f32)
    for part in range(rows // tile):
        span = slice(part * tile, (part + 1) * tile)
        codes = code_one[:, span]
        slot = jnp.sum(
            jnp.where(iota((parents, tile), 0) == codes, slot_col[...], 0), axis=0, keepdims=True
        )
        target = lax.shift_right_logical(slot, book_shift)
        hits = iota((owners, tile), 0) == target
        marks = jnp.where(hits, 1.0, 0.0)
        ranks = dot(marks.astype(bf16), upto) + offset
        offset = offset + jnp.sum(marks, axis=1, keepdims=True)
        place = jnp.sum(
            jnp.where(hits, iota((owners, tile), 0) * cap + ranks.astype(i32) - 1, 0),
            axis=0,
            keepdims=True,
        )
        cell = (slot - target * books) * words + code_two[:, span]
        pos_row[:, span] = place
        pos_col[span, :] = column(place)
        which = iota((16, tile), 0)
        high = lax.shift_right_logical(cell, digit_bits)
        low = cell & (2**digit_bits - 1)
        mixed = jnp.where(which == 0, high, jnp.where(which == 1, low, 1))
        digits[:, span] = mixed.astype(f32).astype(bf16)

    def select(peer):
        return one_hot(iota((cap, rows), 0) + peer * cap == pos_row[...])

    def make_codes(peer):
        sums = lax.dot_general(
            digits[...], select(peer), (((1,), (1,)), ((), ())), preferred_element_type=f32
        )
        code = sums[0:1] * 2.0**digit_bits + sums[1:2] + (sums[2:3] - 1.0)
        return jnp.broadcast_to(code.astype(i32), (8, cap))

    pl.semaphore_wait(barrier, owners - 1)

    @pl.loop(1, owners)
    def _(k):
        peer = other(k)
        send_codes[peer] = make_codes(peer)
        codes_to(peer).start()

    @pl.loop(1, owners)
    def _(k):
        peer = other(k)
        packed[block(peer), :] = dot(select(peer), emb[...]).astype(bf16)
        rows_to(peer).start()

    got_codes[me] = make_codes(me)
    arrived[block(me), :] = dot(select(me), emb[...]).astype(bf16)

    @pl.loop(1, owners)
    def _(k):
        codes_from(other(k)).wait_recv()

    @pl.loop(0, owners)
    def _(s):
        cell_col[block(s), :] = column(got_codes[s][0:1, :])

    @pl.loop(0, slots // tile)
    def _(t):
        cell_row[:, block(t, tile)] = as_row(cell_col[block(t, tile), :])

    span = min(cells, 2048)

    @pl.loop(0, slots // tile)
    def _(t):
        mine = cell_col[block(t, tile), :]
        count = jnp.sum(jnp.where(mine == cell_row[...], 1.0, 0.0), axis=1, keepdims=True)
        shares[block(t, tile), :] = count + prior_two
        found = jnp.zeros((tile, width), f32)
        for at in range(0, cells, span):
            chosen = one_hot(mine - at == iota((tile, span), 1))
            found = found + dot(chosen, cent_two[at : at + span, :])
        picked[block(t, tile), :] = found.astype(bf16)

    @pl.loop(1, owners)
    def _(k):
        rows_from(other(k)).wait_recv()

    marks = jnp.where(
        iota((16, slots), 0) == lax.shift_right_arithmetic(cell_row[...], word_shift), 1.0, 0.0
    )
    sums = dot(marks.astype(bf16), arrived[...])
    tally = jnp.sum(marks, axis=1, keepdims=True)
    held = iota((16, parents), 0)
    chosen = jnp.where((slot_row[...] == held + me * books) & (held < books), 1.0, 0.0)
    own_one[...] = (sums + prior_one * exact_dot(chosen, cent_one[...])) / (tally + prior_one)

    def second(peer):
        mine = cell_col[block(peer), :]
        sums = dot(one_hot(mine == cell_row[...]), arrived[...])
        sums = sums + picked[block(peer), :].astype(f32)
        book = lax.shift_right_arithmetic(mine, word_shift)
        for b in range(books):
            sums = sums + jnp.where(book == b, own_one[b : b + 1, :], 0.0)
        value = arrived[block(peer), :].astype(f32) - sums / shares[block(peer), :]
        return value.astype(bf16)

    @pl.loop(1, owners)
    def _(k):
        peer = other(k)
        outgoing[block(peer), :] = second(peer)
        back_to(peer).start()

    @pl.loop(1, owners)
    def _(k):
        one_copy(me, other(k), other(k)).start()

    all_one[block(me, books), :] = own_one[0:books, :]
    returned[block(me), :] = second(me)

    high = min(words, 512)

    @pl.loop(0, cells // high)
    def _(t):
        base = own_one[pl.ds(t // (words // high), 1), :]
        sums = jnp.zeros((high, width), f32)
        count = jnp.zeros((high, 1), f32)
        half = min(slots, 2048)
        for at in range(0, slots, half):
            marks = jnp.where(
                iota((high, half), 0) + t * high == cell_row[:, at : at + half], 1.0, 0.0
            )
            count = count + jnp.sum(marks, axis=1, keepdims=True)
            sums = sums + dot(marks.astype(bf16), arrived[at : at + half, :])
        old = cent_two[block(t, high), :].astype(f32)
        fresh = (sums - count * base + prior_two * old) / (count + prior_two)
        new_two[block(t, high), :] = fresh.astype(bf16)

    def put_back(peer):
        chosen = one_hot(pos_col[...] - peer * cap == iota((rows, cap), 1))
        return dot(chosen, returned[block(peer), :])

    total[...] = put_back(me)

    @pl.loop(1, owners)
    def _(k):
        peer = other(owners - k)
        back_from(peer).wait_recv()
        total[...] += put_back(peer)

    resid[...] = total[...].astype(bf16)

    @pl.loop(1, owners)
    def _(k):
        peer = other(k)
        one_copy(peer, me, peer).wait_recv()

    new_one[...] = exact_dot(
        jnp.where(slot_col[...] == iota((parents, parents), 1), 1.0, 0.0), all_one[...]
    )

    @pl.loop(1, owners)
    def _(k):
        peer = other(k)
        codes_to(peer).wait_send()
        rows_to(peer).wait_send()
        back_to(peer).wait_send()
        one_copy(me, peer, peer).wait_send()


def shards(embeddings, code_one, code_two, parent_slot, centers_one, centers_two):
    rows, width = embeddings.shape
    owners = lax.axis_size("owner")
    parents = centers_one.shape[0]
    books, words, _ = centers_two.shape
    cells = books * words
    cap = 2 * rows // owners
    slots = owners * cap
    vmem = pl.BlockSpec(memory_space=pltpu.VMEM)
    new_one, new_two, resid = pl.pallas_call(
        functools.partial(kernel, owners, books),
        out_shape=(
            jax.ShapeDtypeStruct((parents, width), f32),
            jax.ShapeDtypeStruct((cells, width), bf16),
            jax.ShapeDtypeStruct((rows, width), bf16),
        ),
        in_specs=[vmem] * 7,
        out_specs=(vmem,) * 3,
        scratch_shapes=[
            pltpu.VMEM((1, rows), i32),
            pltpu.VMEM((rows, 1), i32),
            pltpu.VMEM((16, rows), bf16),
            pltpu.VMEM((owners, 8, cap), i32),
            pltpu.VMEM((owners, 8, cap), i32),
            pltpu.VMEM((slots, 1), i32),
            pltpu.VMEM((1, slots), i32),
            pltpu.VMEM((slots, width), bf16),
            pltpu.VMEM((slots, width), bf16),
            pltpu.VMEM((slots, width), bf16),
            pltpu.VMEM((slots, 1), f32),
            pltpu.VMEM((slots, width), bf16),
            pltpu.VMEM((slots, width), bf16),
            pltpu.VMEM((rows, width), f32),
            pltpu.VMEM((16, width), f32),
            pltpu.VMEM((owners * books, width), f32),
        ]
        + [pltpu.SemaphoreType.DMA((owners,))] * 8,
        compiler_params=pltpu.CompilerParams(
            collective_id=0, has_side_effects=True, vmem_limit_bytes=56 * 2**20
        ),
        name="refine",
    )(
        embeddings,
        code_one.reshape(1, rows),
        code_two.reshape(1, rows),
        parent_slot.reshape(parents, 1),
        parent_slot.reshape(1, parents),
        centers_one,
        centers_two.reshape(cells, width),
    )
    return new_one, new_two.reshape(books, words, width), resid


def solution(mesh):
    placed = (
        P(("groups", "owner"), None),
        P(("groups", "owner")),
        P(("groups", "owner")),
        P("groups"),
        P("groups", None),
        P(("groups", "owner"), None, None),
    )
    return jax.shard_map(
        shards,
        mesh=mesh,
        in_specs=placed,
        out_specs=(
            P("groups", None),
            P(("groups", "owner"), None, None),
            P(("groups", "owner"), None),
        ),
        check_vma=False,
    )
```

```python
import functools

import jax
import jax.numpy as jnp
from jax import lax
from jax.experimental import pallas as pl
from jax.experimental.pallas import tpu as pltpu
from jax.sharding import PartitionSpec as P

prior_one = 16.0
prior_two = 1.0
tile = 256
digit_bits = 7
pieces = 8
bf16 = jnp.bfloat16
f32 = jnp.float32
i32 = jnp.int32


def iota(shape, axis):
    return lax.broadcasted_iota(i32, shape, axis)


def shift_of(count):
    assert count & (count - 1) == 0
    return count.bit_length() - 1


def one_hot(hits):
    return jnp.where(hits, 1.0, 0.0).astype(bf16)


def dot(left, right):
    return jnp.dot(left, right, preferred_element_type=f32)


def exact_dot(left, right):
    return jnp.dot(left, right, preferred_element_type=f32, precision=lax.Precision.HIGHEST)


def column(row):
    size = row.shape[1]
    same = iota((size, size), 0) == iota((size, size), 1)
    return jnp.sum(jnp.where(same, row, 0), axis=1, keepdims=True)


def as_row(col):
    size = col.shape[0]
    same = iota((size, size), 0) == iota((size, size), 1)
    return jnp.sum(jnp.where(same, col, 0), axis=0, keepdims=True)


def kernel(
    owners,
    books,
    emb,
    code_one,
    code_two,
    slot_row,
    cent_one,
    cent_two,
    new_one,
    new_two,
    resid,
    slot_col,
    old_two,
    fresh_two,
    pos_row,
    pos_col,
    digits,
    send_codes,
    got_codes,
    cell_col,
    cell_row,
    packed,
    arrived,
    picked,
    shares,
    outgoing,
    returned,
    total,
    own_one,
    all_one,
    code_send,
    code_recv,
    row_send,
    row_recv,
    back_send,
    back_recv,
    one_send,
    one_recv,
    load_sem,
    save_sem,
    ready,
):
    me = lax.axis_index("owner")
    rows, width = emb.shape
    parents = cent_one.shape[0]
    cells = cent_two.shape[0]
    words = cells // books
    slots = arrived.shape[0]
    cap = slots // owners
    word_shift = shift_of(words)
    book_shift = shift_of(books)

    def other(k):
        return lax.rem(me + owners // 2 + (1 - k % 2 * 2) * (k // 2) + owners, owners)

    def block(index, size=cap):
        return pl.ds(pl.multiple_of(index * size, size), size)

    def codes_to(peer):
        return pltpu.make_async_remote_copy(
            src_ref=send_codes.at[peer],
            dst_ref=got_codes.at[me],
            send_sem=code_send.at[peer],
            recv_sem=code_recv.at[me],
            device_id={"owner": peer},
            device_id_type=pl.DeviceIdType.MESH,
        )

    def codes_from(peer):
        return pltpu.make_async_remote_copy(
            src_ref=send_codes.at[me],
            dst_ref=got_codes.at[peer],
            send_sem=code_send.at[me],
            recv_sem=code_recv.at[peer],
            device_id={"owner": peer},
            device_id_type=pl.DeviceIdType.MESH,
        )

    def block_copy(source, landing, send, recv, source_at, landing_at, peer, size=cap):
        return pltpu.make_async_remote_copy(
            src_ref=source.at[block(source_at, size)],
            dst_ref=landing.at[block(landing_at, size)],
            send_sem=send.at[source_at],
            recv_sem=recv.at[landing_at],
            device_id={"owner": peer},
            device_id_type=pl.DeviceIdType.MESH,
        )

    def rows_to(peer):
        return block_copy(packed, arrived, row_send, row_recv, peer, me, peer)

    def rows_from(peer):
        return block_copy(packed, arrived, row_send, row_recv, me, peer, peer)

    def back_to(peer):
        return block_copy(outgoing, returned, back_send, back_recv, peer, me, peer)

    def back_from(peer):
        return block_copy(outgoing, returned, back_send, back_recv, me, peer, peer)

    def one_copy(landing_at, sem_at, peer):
        return pltpu.make_async_remote_copy(
            src_ref=own_one.at[pl.ds(0, books)],
            dst_ref=all_one.at[block(landing_at, books)],
            send_sem=one_send.at[sem_at],
            recv_sem=one_recv.at[landing_at],
            device_id={"owner": peer},
            device_id_type=pl.DeviceIdType.MESH,
        )

    load_two = pltpu.make_async_copy(cent_two, old_two, load_sem)
    load_two.start()
    barrier = pltpu.get_barrier_semaphore()

    @pl.loop(1, owners)
    def _(k):
        pl.semaphore_signal(
            barrier, inc=1, device_id={"owner": other(k)}, device_id_type=pl.DeviceIdType.MESH
        )

    piece = min(parents, tile)
    for at in range(0, parents, piece):
        slot_col[at : at + piece, :] = column(slot_row[:, at : at + piece])

    upto = one_hot(iota((tile, tile), 0) <= iota((tile, tile), 1))
    offset = jnp.zeros((owners, 1), f32)
    for part in range(rows // tile):
        span = slice(part * tile, (part + 1) * tile)
        codes = code_one[:, span]
        slot = jnp.sum(
            jnp.where(iota((parents, tile), 0) == codes, slot_col[...], 0), axis=0, keepdims=True
        )
        target = lax.shift_right_logical(slot, book_shift)
        hits = iota((owners, tile), 0) == target
        marks = jnp.where(hits, 1.0, 0.0)
        ranks = dot(marks.astype(bf16), upto) + offset
        offset = offset + jnp.sum(marks, axis=1, keepdims=True)
        place = jnp.sum(
            jnp.where(hits, iota((owners, tile), 0) * cap + ranks.astype(i32) - 1, 0),
            axis=0,
            keepdims=True,
        )
        cell = (slot - target * books) * words + code_two[:, span]
        pos_row[:, span] = place
        pos_col[span, :] = column(place)
        which = iota((16, tile), 0)
        high = lax.shift_right_logical(cell, digit_bits)
        low = cell & (2**digit_bits - 1)
        mixed = jnp.where(which == 0, high, jnp.where(which == 1, low, 1))
        digits[:, span] = mixed.astype(f32).astype(bf16)

    def select(peer):
        return one_hot(iota((cap, rows), 0) + peer * cap == pos_row[...])

    def make_codes(peer):
        sums = lax.dot_general(
            digits[...], select(peer), (((1,), (1,)), ((), ())), preferred_element_type=f32
        )
        code = sums[0:1] * 2.0**digit_bits + sums[1:2] + (sums[2:3] - 1.0)
        return jnp.broadcast_to(code.astype(i32), (8, cap))

    pl.semaphore_wait(barrier, owners - 1)

    @pl.loop(1, owners)
    def _(k):
        peer = other(k)
        send_codes[peer] = make_codes(peer)
        codes_to(peer).start()

    @pl.loop(1, owners)
    def _(k):
        peer = other(k)
        packed[block(peer), :] = dot(select(peer), emb[...]).astype(bf16)
        rows_to(peer).start()

    got_codes[me] = make_codes(me)
    arrived[block(me), :] = dot(select(me), emb[...]).astype(bf16)

    @pl.loop(1, owners)
    def _(k):
        codes_from(other(k)).wait_recv()

    @pl.loop(0, owners)
    def _(s):
        cell_col[block(s), :] = column(got_codes[s][0:1, :])

    @pl.loop(0, slots // tile)
    def _(t):
        cell_row[:, block(t, tile)] = as_row(cell_col[block(t, tile), :])

    span = min(cells, 2048)
    load_two.wait()

    @pl.loop(0, slots // tile)
    def _(t):
        mine = cell_col[block(t, tile), :]
        count = jnp.sum(jnp.where(mine == cell_row[...], 1.0, 0.0), axis=1, keepdims=True)
        shares[block(t, tile), :] = count + prior_two
        found = jnp.zeros((tile, width), f32)
        for at in range(0, cells, span):
            chosen = one_hot(mine - at == iota((tile, span), 1))
            found = found + dot(chosen, old_two[at : at + span, :])
        picked[block(t, tile), :] = found.astype(bf16)

    @pl.loop(1, owners)
    def _(k):
        rows_from(other(k)).wait_recv()

    @pl.loop(1, owners)
    def _(k):
        pl.semaphore_signal(
            ready, inc=1, device_id={"owner": other(k)}, device_id_type=pl.DeviceIdType.MESH
        )

    marks = jnp.where(
        iota((16, slots), 0) == lax.shift_right_arithmetic(cell_row[...], word_shift), 1.0, 0.0
    )
    sums = dot(marks.astype(bf16), arrived[...])
    tally = jnp.sum(marks, axis=1, keepdims=True)
    held = iota((16, parents), 0)
    chosen = jnp.where((slot_row[...] == held + me * books) & (held < books), 1.0, 0.0)
    own_one[...] = (sums + prior_one * exact_dot(chosen, cent_one[...])) / (tally + prior_one)

    @pl.loop(1, owners)
    def _(k):
        one_copy(me, other(k), other(k)).start()

    all_one[block(me, books), :] = own_one[0:books, :]

    def second(peer):
        mine = cell_col[block(peer), :]
        sums = dot(one_hot(mine == cell_row[...]), arrived[...])
        sums = sums + picked[block(peer), :].astype(f32)
        book = lax.shift_right_arithmetic(mine, word_shift)
        for b in range(books):
            sums = sums + jnp.where(book == b, own_one[b : b + 1, :], 0.0)
        value = arrived[block(peer), :].astype(f32) - sums / shares[block(peer), :]
        return value.astype(bf16)

    returned[block(me), :] = second(me)
    pl.semaphore_wait(ready, owners - 1)

    @pl.loop(1, owners)
    def _(k):
        peer = other(k)
        outgoing[block(peer), :] = second(peer)
        back_to(peer).start()


    high = min(words, 512)

    def save(t):
        return pltpu.make_async_copy(
            fresh_two.at[block(t, high)], new_two.at[block(t, high)], save_sem.at[t]
        )

    @pl.loop(0, cells // high)
    def _(t):
        base = own_one[pl.ds(t // (words // high), 1), :]
        sums = jnp.zeros((high, width), f32)
        count = jnp.zeros((high, 1), f32)
        half = min(slots, 2048)
        for at in range(0, slots, half):
            marks = jnp.where(
                iota((high, half), 0) + t * high == cell_row[:, at : at + half], 1.0, 0.0
            )
            count = count + jnp.sum(marks, axis=1, keepdims=True)
            sums = sums + dot(marks.astype(bf16), arrived[at : at + half, :])
        old = old_two[block(t, high), :].astype(f32)
        fresh = (sums - count * base + prior_two * old) / (count + prior_two)
        fresh_two[block(t, high), :] = fresh.astype(bf16)
        save(t).start()

    def put_back(peer):
        chosen = one_hot(pos_col[...] - peer * cap == iota((rows, cap), 1))
        return dot(chosen, returned[block(peer), :])

    total[...] = put_back(me)

    @pl.loop(1, owners)
    def _(k):
        peer = other(k)
        back_from(peer).wait_recv()
        total[...] += put_back(peer)

    resid[...] = total[...].astype(bf16)

    @pl.loop(1, owners)
    def _(k):
        peer = other(k)
        one_copy(peer, me, peer).wait_recv()

    new_one[...] = exact_dot(
        jnp.where(slot_col[...] == iota((parents, parents), 1), 1.0, 0.0), all_one[...]
    )

    @pl.loop(1, owners)
    def _(k):
        peer = other(k)
        codes_to(peer).wait_send()
        rows_to(peer).wait_send()
        back_to(peer).wait_send()
        one_copy(me, peer, peer).wait_send()

    @pl.loop(0, cells // high)
    def _(t):
        save(t).wait()


def hand_on(one_in, two_in, resid_in, one_out, two_out, resid_out, one, two, resid, loads, saves):
    part = two_in.shape[0] // pieces
    moves = [(resid_in, resid, resid_out), (one_in, one, one_out)]
    for i in range(pieces):
        span = pl.ds(i * part, part)
        moves.append((two_in.at[span], two.at[span], two_out.at[span]))
    into = [
        pltpu.make_async_copy(move[0], move[1], loads.at[i]) for i, move in enumerate(moves)
    ]
    out_of = [
        pltpu.make_async_copy(move[1], move[2], saves.at[i]) for i, move in enumerate(moves)
    ]
    for copy in into:
        copy.start()
    for first, then in zip(into, out_of):
        first.wait()
        then.start()
    for copy in out_of:
        copy.wait()


def shards(embeddings, code_one, code_two, parent_slot, centers_one, centers_two):
    rows, width = embeddings.shape
    owners = lax.axis_size("owner")
    parents = centers_one.shape[0]
    books, words, _ = centers_two.shape
    cells = books * words
    cap = 2 * rows // owners
    slots = owners * cap
    vmem = pl.BlockSpec(memory_space=pltpu.VMEM)
    new_one, new_two, resid = pl.pallas_call(
        functools.partial(kernel, owners, books),
        out_shape=(
            jax.ShapeDtypeStruct((parents, width), f32),
            jax.ShapeDtypeStruct((cells, width), bf16),
            jax.ShapeDtypeStruct((rows, width), bf16),
        ),
        in_specs=[vmem] * 5 + [pl.BlockSpec(memory_space=pl.ANY)],
        out_specs=(vmem, pl.BlockSpec(memory_space=pl.ANY), vmem),
        scratch_shapes=[
            pltpu.VMEM((parents, 1), i32),
            pltpu.VMEM((cells, width), bf16),
            pltpu.VMEM((cells, width), bf16),
            pltpu.VMEM((1, rows), i32),
            pltpu.VMEM((rows, 1), i32),
            pltpu.VMEM((16, rows), bf16),
            pltpu.VMEM((owners, 8, cap), i32),
            pltpu.VMEM((owners, 8, cap), i32),
            pltpu.VMEM((slots, 1), i32),
            pltpu.VMEM((1, slots), i32),
            pltpu.VMEM((slots, width), bf16),
            pltpu.VMEM((slots, width), bf16),
            pltpu.VMEM((slots, width), bf16),
            pltpu.VMEM((slots, 1), f32),
            pltpu.VMEM((slots, width), bf16),
            pltpu.VMEM((slots, width), bf16),
            pltpu.VMEM((rows, width), f32),
            pltpu.VMEM((16, width), f32),
            pltpu.VMEM((owners * books, width), f32),
        ]
        + [pltpu.SemaphoreType.DMA((owners,))] * 8
        + [pltpu.SemaphoreType.DMA, pltpu.SemaphoreType.DMA((cells // min(words, 512),))]
        + [pltpu.SemaphoreType.REGULAR],
        compiler_params=pltpu.CompilerParams(
            collective_id=0, has_side_effects=True, vmem_limit_bytes=56 * 2**20
        ),
        name="refine",
    )(
        embeddings,
        code_one.reshape(1, rows),
        code_two.reshape(1, rows),
        parent_slot.reshape(1, parents),
        centers_one,
        centers_two.reshape(cells, width),
    )
    hbm = pl.BlockSpec(memory_space=pl.ANY)
    results = (new_one, new_two, resid)
    new_one, new_two, resid = pl.pallas_call(
        hand_on,
        out_shape=tuple(jax.ShapeDtypeStruct(x.shape, x.dtype) for x in results),
        in_specs=[hbm] * 3,
        out_specs=(hbm,) * 3,
        scratch_shapes=[pltpu.VMEM(x.shape, x.dtype) for x in results]
        + [pltpu.SemaphoreType.DMA((2 + pieces,))] * 2,
        compiler_params=pltpu.CompilerParams(vmem_limit_bytes=56 * 2**20),
        name="hand_on",
    )(*results)
    return new_one, new_two.reshape(books, words, width), resid


def solution(mesh):
    placed = (
        P(("groups", "owner"), None),
        P(("groups", "owner")),
        P(("groups", "owner")),
        P("groups"),
        P("groups", None),
        P(("groups", "owner"), None, None),
    )
    return jax.shard_map(
        shards,
        mesh=mesh,
        in_specs=placed,
        out_specs=(
            P("groups", None),
            P(("groups", "owner"), None, None),
            P(("groups", "owner"), None),
        ),
        check_vma=False,
    )
```
